32 devices in a mesh: groups: 2 (over x), expert: 16 (over z, y, core).
Axes of the slice: x: 2, y: 2, z: 4, core: 2. Of those that a mesh axis runs over, the one named last changes fastest.
Arguments:
- tokens: bfloat16 [512, 2048], P(('groups', 'expert')), parts along dimension 0, may hold values from -6 to 6
- tangent: bfloat16 [512, 2048], P(('groups', 'expert')), parts along dimension 0, may hold values from -6 to 6
- cotangent: bfloat16 [512, 2048], P(('groups', 'expert')), parts along dimension 0, may hold values from -6 to 6
- routes: int32 [512, 8], P(('groups', 'expert')), parts along dimension 0, may hold values from 0 to 15, as said below
- route_weight: bfloat16 [512, 8], P(('groups', 'expert')), parts along dimension 0, may hold values from 0.099609375 to 1
- gate_weight: bfloat16 [16, 2048, 768], P('expert'), may hold values from -0.125 to 0.125
- up_weight: bfloat16 [16, 2048, 768], P('expert'), may hold values from -0.125 to 0.125
- down_weight: bfloat16 [16, 768, 2048], P('expert'), may hold values from -0.21875 to 0.21875
Outputs:
- hvp: float32 [512, 2048], P(('groups', 'expert')), parts along dimension 0
The draws below stay inside these ranges and needn't reach their ends.
There are 2 independent parts, one for each index of `groups`. The reference program is written for one: setup_inputs(seed, part) draws one part's arguments, and reference() takes and returns one part's arrays. A program takes and returns all parts, laid end to end along the dimension named above; an argument that names none is the same for every part. Nothing has to cross between parts.
Inputs may be any that keep to these rules, and one draw needn't show every extreme that they name: `routes`: each row names 8 different experts. Among the rows of one device no expert is named more than 16 times, and one expert is named exactly 16 times among the rows of every device.
All inputs are finite; a program needn't handle non-finite values.
Results may differ from the reference program's by a relative error of at most 0.004.
Values may be sent and summed in bfloat16 or wider, within the bound.
A program may use at most 64 MiB of HBM per device.

```python
import math
import jax
import jax.numpy as jnp
from jax import lax

D = 2048
F = 768
TOP = 8
TOK_DEV = 16
EXPERTS = 16
TOKENS = 256
CAP = 16


def draw_routes(key, part):
    key = jax.random.fold_in(key, 7)
    hottest = jax.random.randint(jax.random.fold_in(key, 1), (), 0, EXPERTS)
    token_pos = jnp.arange(TOK_DEV, dtype=jnp.int32)[:, None]
    route_pos = jnp.arange(TOP, dtype=jnp.int32)[None, :]
    is_hot = (route_pos == 0) & (token_pos < CAP)
    before = jnp.minimum(token_pos, CAP) + ((route_pos > 0) & (token_pos < CAP)).astype(jnp.int32)
    remaining = token_pos * TOP + route_pos - before

    def one_block(block_id):
        block_key = jax.random.fold_in(key, 100 + block_id)
        others = jax.random.permutation(jax.random.fold_in(block_key, 1), EXPERTS - 1).astype(jnp.int32)
        others = others + (others >= hottest).astype(jnp.int32)
        modulus = jax.random.randint(jax.random.fold_in(block_key, 2), (), EXPERTS // 2, EXPERTS)
        picked = jnp.where(is_hot, hottest, others[jnp.maximum(remaining, 0) % modulus])
        order = jax.random.permutation(jax.random.fold_in(block_key, 3), TOK_DEV)
        return picked[order]
    blocks = jax.vmap(one_block)(jnp.arange(TOKENS // TOK_DEV, dtype=jnp.int32))
    return blocks.reshape(TOKENS, TOP).astype(jnp.int32)


def block_scale(own_key, extent, shards, least, largest):
    def one(position, parts):
        draws = jax.random.uniform(jax.random.fold_in(jax.random.fold_in(own_key, 6), position), (parts,), jnp.float32, least / len(shards), largest / len(shards))
        return jnp.repeat(jnp.exp(draws), extent[position] // parts).reshape((-1,) + (1,) * (len(extent) - position - 1))

    level = one(*shards[0])
    for cut in shards[1:]:
        level = level * one(*cut)
    return level


def gaussian(own_key, shape, deviation, most, pieces=(), kind=jnp.bfloat16):
    entries = deviation * jax.random.normal(own_key, shape, jnp.float32)
    if pieces:
        entries = entries * block_scale(own_key, shape, pieces, -0.22, 0.18)
    return jnp.clip(entries, -most, most).astype(kind)


def setup_inputs(seed: int = 0, part: int = 0) -> dict:
    streams_of = jax.random.split(jax.random.key(seed), 9)
    part_keys = jax.random.split(jax.random.fold_in(streams_of[8], part), 9)
    tokens = gaussian(part_keys[0], (TOKENS, D), 1.0, 6.0, ((0, 16),))
    tangent = gaussian(part_keys[1], (TOKENS, D), 1.0, 6.0, ((0, 16),))
    cotangent = gaussian(part_keys[2], (TOKENS, D), 1.0, 6.0, ((0, 16),))
    routes = draw_routes(jax.random.fold_in(jax.random.fold_in(streams_of[8], part), 71), part)
    route_weight = jnp.clip(jnp.exp(math.log(1.0) - 2.306499 * jax.random.uniform(part_keys[4], (TOKENS, TOP), jnp.float32) ** block_scale(part_keys[4], (TOKENS, TOP), ((0, 16),), -0.2, 0.2)), 0.099609375, 1.0).astype(jnp.bfloat16)
    gate_weight = gaussian(streams_of[5], (EXPERTS, D, F), D ** -0.5, 0.125, ((0, 16),))
    up_weight = gaussian(streams_of[6], (EXPERTS, D, F), D ** -0.5, 0.125, ((0, 16),))
    down_weight = gaussian(streams_of[7], (EXPERTS, F, D), F ** -0.5, 0.21875, ((0, 16),))
    return {"tokens": tokens, "tangent": tangent, "cotangent": cotangent, "routes": routes, "route_weight": route_weight, "gate_weight": gate_weight, "up_weight": up_weight, "down_weight": down_weight}


def expert_term(rows_x, rows_v, rows_c, rows_w, gate_w, up_w, down_w):
    gate = jnp.dot(rows_x, gate_w, preferred_element_type=jnp.float32)
    upper = jnp.dot(rows_x, up_w, preferred_element_type=jnp.float32)
    gate_dot = jnp.dot(rows_v, gate_w, preferred_element_type=jnp.float32)
    up_dot = jnp.dot(rows_v, up_w, preferred_element_type=jnp.float32)
    back = lax.dot_general(rows_c, down_w, (((1,), (1,)), ((), ())), preferred_element_type=jnp.float32)
    back = back * rows_w[:, None]
    sigma = jax.nn.sigmoid(gate)
    first = sigma * (1.0 + gate * (1.0 - sigma))
    second = sigma * (1.0 - sigma) * (2.0 + gate * (1.0 - 2.0 * sigma))
    gate_change = (back * (up_dot * first + upper * second * gate_dot)).astype(jnp.bfloat16)
    up_change = (back * first * gate_dot).astype(jnp.bfloat16)
    term = lax.dot_general(gate_change, gate_w, (((1,), (1,)), ((), ())), preferred_element_type=jnp.float32)
    term = term + lax.dot_general(up_change, up_w, (((1,), (1,)), ((), ())), preferred_element_type=jnp.float32)
    return term.astype(jnp.bfloat16)


def reference(tokens, tangent, cotangent, routes, route_weight, gate_weight, up_weight, down_weight):
    flat_routes = routes.reshape(-1)
    flat_weights = route_weight.reshape(-1).astype(jnp.float32)
    limit = EXPERTS * CAP

    def visit(running, expert_id):
        chosen = flat_routes == expert_id
        counted = jnp.sum(chosen.astype(jnp.int32))
        where_idx = jnp.nonzero(chosen, size=limit, fill_value=0)[0].astype(jnp.int32)
        live = jnp.arange(limit, dtype=jnp.int32) < counted
        weights = jnp.where(live, flat_weights[where_idx], jnp.float32(0.0))
        owners = (where_idx // TOP).astype(jnp.int32)
        term = expert_term(tokens[owners], tangent[owners], cotangent[owners], weights,
                           gate_weight[expert_id], up_weight[expert_id], down_weight[expert_id])
        running = running.at[owners].add(term.astype(jnp.float32))
        return running, None

    start_sum = jnp.zeros((TOKENS, D), jnp.float32)
    result, _ = lax.scan(visit, start_sum, jnp.arange(EXPERTS, dtype=jnp.int32))
    return result
```

```python
import functools

import jax
import jax.numpy as jnp
from jax import lax
from jax.experimental import pallas as pl
from jax.experimental.pallas import tpu as pltpu
from jax.sharding import PartitionSpec as P

LANES = 128
BF16 = jnp.bfloat16
F32 = jnp.float32
NT = (((1,), (1,)), ((), ()))


def whole_block_kernel(
    lines, parts,
    x_hbm, v_hbm, c_hbm, routes_ref, rw_ref, g_hbm, u_hbm, d_hbm, out_ref,
    xv, cw, g, u, d, a_s, b_s, gc, uc, term, q,
    s1, r1, s2, r2, su, ru, sd, rd,
    local, zs, zr, ys, yr, ss, sr, rs_s, rs_r, us, ur, ds_, dr,
):
    rows, width = x_hbm.shape
    hidden = g.shape[1]
    total = lines * 4 * rows
    piece = width // parts
    me = lax.axis_index("expert")
    core = lax.rem(me, 2)
    y = lax.rem(lax.div(me, 2), 2)
    z = lax.div(me, 4)
    last = lines - 1

    def dev(zz, yy, cc):
        return (zz * 2 + yy) * 2 + cc

    sib = dev(z, y, 1 - core)
    ynb = dev(z, 1 - y, core)

    def remote(src, dst, send, recv, target):
        return pltpu.make_async_remote_copy(
            src_ref=src, dst_ref=dst, send_sem=send, recv_sem=recv,
            device_id={"expert": target}, device_id_type=pl.DeviceIdType.MESH,
        )

    loads = [
        pltpu.make_async_copy(x_hbm, xv.at[0, me], local.at[0]),
        pltpu.make_async_copy(v_hbm, xv.at[1, me], local.at[1]),
        pltpu.make_async_copy(c_hbm, cw.at[me, :, pl.ds(0, width)], local.at[2]),
        pltpu.make_async_copy(g_hbm.at[0], g, local.at[3]),
        pltpu.make_async_copy(u_hbm.at[0], u, local.at[4]),
        pltpu.make_async_copy(d_hbm.at[0], d, local.at[5]),
    ]
    for load in loads:
        load.start()

    barrier = pltpu.get_barrier_semaphore()

    def greet(target):
        pl.semaphore_signal(
            barrier, inc=1, device_id={"expert": target}, device_id_type=pl.DeviceIdType.MESH
        )

    greet(sib)
    greet(ynb)

    @pl.when(z > 0)
    def _():
        greet(me - 4)

    @pl.when(z < last)
    def _():
        greet(me + 4)

    lane = lax.broadcasted_iota(jnp.int32, (rows, LANES), 1)
    routes = routes_ref[...]
    weights = rw_ref[...].astype(F32)
    table = jnp.zeros((rows, LANES), F32)
    for k in range(routes.shape[1]):
        table = table + jnp.where(routes[:, k : k + 1] == lane, weights[:, k : k + 1], 0.0)
    cw[me, :, width:] = table.astype(BF16)

    pl.semaphore_wait(barrier, 2 + (z > 0).astype(jnp.int32) + (z < last).astype(jnp.int32))

    def block(p, index):
        return xv.at[:, index] if p == 0 else cw.at[index]

    def zcopy(p, way, s):
        ref = block(p, dev(s, y, core))
        return remote(ref, ref, zs.at[p, way, s], zr.at[p, way, s], me + 4 if way == 0 else me - 4)

    def ycopy(p, s, col):
        ref = block(p, dev(s, col, core))
        return remote(ref, ref, ys.at[p, s], yr.at[p, s], ynb)

    def scopy(p, k, plane):
        ref = block(p, k * 2 + plane)
        return remote(ref, ref, ss.at[p, k], sr.at[p, k], sib)

    def pass_on(p, s, ways):
        for way in ways:
            @pl.when(z < last if way == 0 else z > 0)
            def _():
                zcopy(p, way, s).start()
        ycopy(p, s, y).start()
        scopy(p, s * 2 + y, core).start()

    def near(t, fn):
        @pl.when(z >= t)
        def _():
            fn(0, z - t)

        @pl.when(z + t <= last)
        def _():
            fn(1, z + t)

    def hop(p, t):
        def arrive(way, s):
            zcopy(p, way, s).wait_recv()
            pass_on(p, s, (way,))
        near(t, arrive)

    def across(p, t):
        def arrive(way, s):
            ycopy(p, s, 1 - y).wait_recv()
            scopy(p, s * 2 + 1 - y, core).start()
        if t == 0:
            arrive(0, z)
        else:
            near(t, arrive)

    def from_sibling(p):
        for k in range(lines * 2):
            scopy(p, k, 1 - core).wait_recv()

    loads[0].wait()
    loads[1].wait()
    pass_on(0, z, (0, 1))
    loads[2].wait()
    for t in range(1, lines):
        hop(0, t)
        across(0, t - 1)
        if t == max(lines - 2, 1):
            pass_on(1, z, (0, 1))
    across(0, last)
    loads[3].wait()
    loads[4].wait()
    from_sibling(0)

    tile = 256
    tiles = hidden // tile
    both = 2 * total
    for n in range(tiles):
        cols = slice(n * tile, (n + 1) * tile)
        stacked = xv[...].reshape(both, width)
        gate_both = jnp.dot(stacked, g[:, cols], preferred_element_type=F32)
        up_both = jnp.dot(stacked, u[:, cols], preferred_element_type=F32)
        gate, gate_dot = gate_both[:total], gate_both[total:]
        upper, up_dot = up_both[:total], up_both[total:]
        sigma = jax.nn.sigmoid(gate)
        first = sigma * (1.0 + gate * (1.0 - sigma))
        second = sigma * (1.0 - sigma) * (2.0 + gate * (1.0 - 2.0 * sigma))
        a_s[:, cols] = up_dot * first + upper * second * gate_dot
        b_s[:, cols] = first * gate_dot
        if n + 1 < lines:
            hop(1, n + 1)
            across(1, n)
    for t in range(tiles + 1, lines):
        hop(1, t)
        across(1, t - 1)
    for t in range(min(tiles, last), lines):
        across(1, t)
    loads[5].wait()
    from_sibling(1)

    tags = cw[:, :, width:].reshape(total, LANES).astype(F32)
    mine = lax.broadcasted_iota(jnp.int32, (total, LANES), 1) == me
    scale = jnp.sum(jnp.where(mine, tags, 0.0), axis=1, keepdims=True)
    for n in range(tiles):
        cols = slice(n * tile, (n + 1) * tile)
        back = lax.dot_general(
            cw[:, :, :width].reshape(total, width), d[cols, :], NT, preferred_element_type=F32
        )
        back = back * scale
        gc[:, cols] = (back * a_s[:, cols]).astype(BF16)
        uc[:, cols] = (back * b_s[:, cols]).astype(BF16)

    def to_sibling(j):
        return remote(s1.at[j], r1.at[j], rs_s.at[0, j], rs_r.at[0, j], sib)

    def to_column(j):
        return remote(s2.at[j], r2.at[j], rs_s.at[1, j], rs_r.at[1, j], ynb)

    def up_copy(j, zd):
        return remote(su.at[j, zd], ru.at[j, zd], us.at[j, zd], ur.at[j, zd], me + 4)

    def down_copy(j, zd):
        return remote(sd.at[j, zd], rd.at[j, zd], ds_.at[j, zd], dr.at[j, zd], me - 4)

    def make_terms(j):
        cols = slice(j * piece, (j + 1) * piece)
        t = lax.dot_general(gc[...], g[cols, :], NT, preferred_element_type=F32)
        t = t + lax.dot_general(uc[...], u[cols, :], NT, preferred_element_type=F32)
        term[j] = t.reshape(lines * 4, rows, piece)
        for k in range(lines * 2):
            s1[j, k] = term[j, 2 * k + 1 - core].astype(BF16)
        to_sibling(j).start()

    def add_sibling(j):
        to_sibling(j).wait_recv()
        for zz in range(lines):
            s2[j, zz] = (
                term[j, dev(zz, 1 - y, core)] + r1[j, zz * 2 + 1 - y].astype(F32)
            ).astype(BF16)
        to_column(j).start()
        for zz in range(lines):
            q[j, zz] = term[j, dev(zz, y, core)] + r1[j, zz * 2 + y].astype(F32)

    def add_column(j):
        to_column(j).wait_recv()
        for zz in range(lines):
            q[j, zz] = q[j, zz] + r2[j, zz].astype(F32)

    def wave(w, j):
        @pl.when(z == w)
        def _():
            for zd in range(last, w, -1):
                total_up = q[j, zd]
                if w > 0:
                    up_copy(j, zd).wait_recv()
                    total_up = total_up + ru[j, zd].astype(F32)
                su[j, zd] = total_up.astype(BF16)
                up_copy(j, zd).start()

        @pl.when(z == last - w)
        def _():
            for zd in range(0, last - w):
                total_down = q[j, zd]
                if w > 0:
                    down_copy(j, zd).wait_recv()
                    total_down = total_down + rd[j, zd].astype(F32)
                sd[j, zd] = total_down.astype(BF16)
                down_copy(j, zd).start()

    for j in range(parts):
        make_terms(j)
        if j > 0:
            add_sibling(j - 1)
        if j > 1:
            add_column(j - 2)
            wave(0, j - 2)
    add_sibling(parts - 1)
    for j in range(max(parts - 2, 0), parts):
        add_column(j)
        wave(0, j)
    for w in range(1, last):
        for j in range(parts):
            wave(w, j)
    for j in range(parts):
        cols = slice(j * piece, (j + 1) * piece)
        out_ref[:, cols] = q[j, z]

        @pl.when(z > 0)
        def _():
            up_copy(j, z).wait_recv()
            out_ref[:, cols] += ru[j, z].astype(F32)

        @pl.when(z < last)
        def _():
            down_copy(j, z).wait_recv()
            out_ref[:, cols] += rd[j, z].astype(F32)

    for p in range(2):
        for way in (0, 1):
            @pl.when(z < last if way == 0 else z > 0)
            def _():
                zcopy(p, way, z).wait_send()
        ycopy(p, z, y).wait_send()
        scopy(p, z * 2 + y, core).wait_send()
        scopy(p, z * 2 + 1 - y, core).wait_send()
        for t in range(1, lines):
            def gone(way, s):
                @pl.when(z < last if way == 0 else z > 0)
                def _():
                    zcopy(p, way, s).wait_send()
                ycopy(p, s, y).wait_send()
                scopy(p, s * 2 + y, core).wait_send()
                scopy(p, s * 2 + 1 - y, core).wait_send()
            near(t, gone)
    for j in range(parts):
        to_sibling(j).wait_send()
        to_column(j).wait_send()
        for zd in range(lines):
            @pl.when(z < zd)
            def _():
                up_copy(j, zd).wait_send()

            @pl.when(z > zd)
            def _():
                down_copy(j, zd).wait_send()


def whole_blocks(x, v, c, routes, rw, g, u, d):
    rows, width = x.shape
    hidden = g.shape[2]
    lines = lax.axis_size("expert") // 4
    blocks = lines * 4
    total = blocks * rows
    parts = 4
    piece = width // parts
    dma = pltpu.SemaphoreType.DMA
    anywhere = pl.BlockSpec(memory_space=pl.ANY)
    vmem = pl.BlockSpec(memory_space=pltpu.VMEM)
    return pl.pallas_call(
        functools.partial(whole_block_kernel, lines, parts),
        out_shape=jax.ShapeDtypeStruct((rows, width), F32),
        in_specs=[anywhere] * 3 + [vmem] * 2 + [anywhere] * 3,
        out_specs=vmem,
        scratch_shapes=[
            pltpu.VMEM((2, blocks, rows, width), BF16),
            pltpu.VMEM((blocks, rows, width + LANES), BF16),
            pltpu.VMEM((width, hidden), BF16),
            pltpu.VMEM((width, hidden), BF16),
            pltpu.VMEM((hidden, width), BF16),
            pltpu.VMEM((total, hidden), F32),
            pltpu.VMEM((total, hidden), F32),
            pltpu.VMEM((total, hidden), BF16),
            pltpu.VMEM((total, hidden), BF16),
            pltpu.VMEM((parts, blocks, rows, piece), F32),
            pltpu.VMEM((parts, lines, rows, piece), F32),
            pltpu.VMEM((parts, lines * 2, rows, piece), BF16),
            pltpu.VMEM((parts, lines * 2, rows, piece), BF16),
            pltpu.VMEM((parts, lines, rows, piece), BF16),
            pltpu.VMEM((parts, lines, rows, piece), BF16),
            pltpu.VMEM((parts, lines, rows, piece), BF16),
            pltpu.VMEM((parts, lines, rows, piece), BF16),
            pltpu.VMEM((parts, lines, rows, piece), BF16),
            pltpu.VMEM((parts, lines, rows, piece), BF16),
            dma((6,)),
            dma((2, 2, lines)),
            dma((2, 2, lines)),
            dma((2, lines)),
            dma((2, lines)),
            dma((2, lines * 2)),
            dma((2, lines * 2)),
            dma((2, parts)),
            dma((2, parts)),
            dma((parts, lines)),
            dma((parts, lines)),
            dma((parts, lines)),
            dma((parts, lines)),
        ],
        compiler_params=pltpu.CompilerParams(
            collective_id=0, has_side_effects=True, vmem_limit_bytes=48 * 2**20
        ),
        cost_estimate=pl.CostEstimate(
            flops=14 * total * width * hidden,
            bytes_accessed=6 * width * hidden + 10 * rows * width,
            transcendentals=total * hidden,
        ),
    )(x, v, c, routes, rw, g, u, d)


def route_terms(rows_x, rows_v, rows_c, rows_w, gate_w, up_w, down_w):
    count = rows_x.shape[0]
    stacked = jnp.concatenate([rows_x, rows_v], axis=0)
    gate_both = jnp.dot(stacked, gate_w, preferred_element_type=jnp.float32)
    up_both = jnp.dot(stacked, up_w, preferred_element_type=jnp.float32)
    gate = gate_both[:count]
    gate_dot = gate_both[count:]
    upper = up_both[:count]
    up_dot = up_both[count:]
    back = lax.dot_general(
        rows_c, down_w, (((1,), (1,)), ((), ())), preferred_element_type=jnp.float32
    )
    back = back * rows_w.astype(jnp.float32)[:, None]
    sigma = jax.nn.sigmoid(gate)
    first = sigma * (1.0 + gate * (1.0 - sigma))
    second = sigma * (1.0 - sigma) * (2.0 + gate * (1.0 - 2.0 * sigma))
    gate_change = (back * (up_dot * first + upper * second * gate_dot)).astype(jnp.bfloat16)
    up_change = (back * first * gate_dot).astype(jnp.bfloat16)
    term = lax.dot_general(
        gate_change, gate_w, (((1,), (1,)), ((), ())), preferred_element_type=jnp.float32
    )
    term = term + lax.dot_general(
        up_change, up_w, (((1,), (1,)), ((), ())), preferred_element_type=jnp.float32
    )
    return term.astype(jnp.bfloat16)


def shards(tokens, tangent, cotangent, routes, route_weight, gate_weight, up_weight, down_weight):
    experts = lax.axis_size("expert")
    tok_rows, width = tokens.shape
    top_count = routes.shape[1]
    slots = 2 * tok_rows * top_count // experts
    if slots >= tok_rows and experts % 4 == 0 and experts <= LANES:
        return whole_blocks(
            tokens, tangent, cotangent, routes, route_weight, gate_weight, up_weight, down_weight
        )
    routed = tok_rows * top_count
    flat_routes = routes.reshape(-1)
    onehot = (flat_routes[:, None] == jnp.arange(experts, dtype=jnp.int32)[None, :]).astype(
        jnp.int32
    )
    slot_rank = jnp.sum((jnp.cumsum(onehot, axis=0) - onehot) * onehot, axis=1)
    target = flat_routes * slots + slot_rank
    source = (
        jnp.zeros((experts * slots,), jnp.int32).at[target].set(jnp.arange(routed, dtype=jnp.int32))
    )
    filled = jnp.zeros((experts * slots,), jnp.bool_).at[target].set(True)
    owner = source // top_count

    def place(values):
        picked = jnp.where(filled[:, None], values[owner], jnp.zeros((), values.dtype))
        return picked.reshape(experts, slots, width)

    send_x = place(tokens)
    send_v = place(tangent)
    send_c = place(cotangent)
    send_w = jnp.where(
        filled, route_weight.reshape(-1)[source], jnp.zeros((), route_weight.dtype)
    ).reshape(experts, slots)
    gate_w = gate_weight[0]
    up_w = up_weight[0]
    down_w = down_weight[0]
    recv_w = lax.all_to_all(send_w, "expert", split_axis=0, concat_axis=0, tiled=True)
    sources, levels = recv_w.shape
    result = route_terms(
        lax.all_to_all(send_x, "expert", split_axis=0, concat_axis=0, tiled=True).reshape(
            -1, width
        ),
        lax.all_to_all(send_v, "expert", split_axis=0, concat_axis=0, tiled=True).reshape(
            -1, width
        ),
        lax.all_to_all(send_c, "expert", split_axis=0, concat_axis=0, tiled=True).reshape(
            -1, width
        ),
        recv_w.reshape(-1),
        gate_w,
        up_w,
        down_w,
    )
    terms = result.reshape(sources, levels, width)
    returned = lax.all_to_all(terms, "expert", split_axis=0, concat_axis=0, tiled=True)
    back_flat = returned.reshape(experts * slots, width)
    per_route = back_flat[target].astype(jnp.float32).reshape(tok_rows, top_count, width)
    return jnp.sum(per_route, axis=1)


def solution(mesh):
    placed = (
        P(("groups", "expert"), None),
        P(("groups", "expert"), None),
        P(("groups", "expert"), None),
        P(("groups", "expert"), None),
        P(("groups", "expert"), None),
        P("expert", None, None),
        P("expert", None, None),
        P("expert", None, None),
    )
    return jax.shard_map(
        shards, mesh=mesh, in_specs=placed, out_specs=P(("groups", "expert"), None), check_vma=False
    )
```

```python
import jax
import jax.numpy as jnp
from jax import lax
from jax.experimental import pallas as pl
from jax.experimental.pallas import tpu as pltpu
from jax.sharding import PartitionSpec as P

LANES = 128
LINES = 4
BF16 = jnp.bfloat16
F32 = jnp.float32
NT = (((1,), (1,)), ((), ()))


def whole_block_kernel(
    x_hbm, v_hbm, c_hbm, routes_ref, rw_ref, g_hbm, u_hbm, d_hbm, out_ref,
    xv, cw, g, u, d, a_s, b_s, gc, uc, term, q,
    s1, r1, s2, r2, sq, rq,
    local, zs, zr, ys, yr, ss, sr, sib_s, sib_r, col_s, col_r, line_s, line_r,
):
    rows, width = x_hbm.shape
    hidden = g.shape[1]
    lines = LINES
    last = lines - 1
    half = lines * 2 * rows
    parts = term.shape[1]
    piece = width // parts
    me = lax.axis_index("expert")
    core = lax.rem(me, 2)
    y = lax.rem(lax.div(me, 2), 2)
    z = lax.div(me, 4)
    pair = lax.div(z, 2)
    low = lax.rem(z, 2)
    base = (2 * pair, 2 * (1 - pair))

    def dev(zz, yy, cc):
        return (zz * 2 + yy) * 2 + cc

    sib = dev(z, y, 1 - core)
    ynb = dev(z, 1 - y, core)

    def remote(src, dst, send, recv, target):
        return pltpu.make_async_remote_copy(
            src_ref=src, dst_ref=dst, send_sem=send, recv_sem=recv,
            device_id={"expert": target}, device_id_type=pl.DeviceIdType.MESH,
        )

    loads = [
        pltpu.make_async_copy(x_hbm, xv.at[0, me], local.at[0]),
        pltpu.make_async_copy(v_hbm, xv.at[1, me], local.at[1]),
        pltpu.make_async_copy(c_hbm, cw.at[me, :, pl.ds(0, width)], local.at[2]),
        pltpu.make_async_copy(g_hbm.at[0], g, local.at[3]),
        pltpu.make_async_copy(u_hbm.at[0], u, local.at[4]),
        pltpu.make_async_copy(d_hbm.at[0], d, local.at[5]),
    ]
    for load in loads:
        load.start()

    barrier = pltpu.get_barrier_semaphore()
    peers = [sib, ynb] + [dev(lax.rem(z + o, lines), y, core) for o in range(1, lines)]
    for peer in peers:
        pl.semaphore_signal(
            barrier, inc=1, device_id={"expert": peer}, device_id_type=pl.DeviceIdType.MESH
        )

    lane = lax.broadcasted_iota(jnp.int32, (rows, LANES), 1)
    eye = lax.broadcasted_iota(jnp.int32, (rows, rows), 0) == lax.broadcasted_iota(
        jnp.int32, (rows, rows), 1
    )
    routes = routes_ref[...].astype(F32)
    weights = rw_ref[...].astype(F32)
    table = jnp.zeros((rows, LANES), F32)
    for k in range(routes.shape[0]):
        route = jnp.sum(jnp.where(eye, routes[k : k + 1, :], 0.0), axis=1, keepdims=True)
        weight = jnp.sum(jnp.where(eye, weights[k : k + 1, :], 0.0), axis=1, keepdims=True)
        table = table + jnp.where(route.astype(jnp.int32) == lane, weight, 0.0)
    cw[me, :, width:] = table.astype(BF16)

    pl.semaphore_wait(barrier, len(peers))

    def block(p, index):
        return cw.at[index] if p == 2 else xv.at[p, index]

    def zcopy(p, way, s, reach=1):
        ref = block(p, dev(s, y, core))
        step = 4 * reach
        target = me + step if way == 0 else me - step
        return remote(ref, ref, zs.at[p, way, s, reach // 2], zr.at[p, way, s], target)

    def ycopy(p, s, col):
        ref = block(p, dev(s, col, core))
        return remote(ref, ref, ys.at[p, s], yr.at[p, s], ynb)

    def scopy(p, k, plane):
        ref = block(p, k * 2 + plane)
        return remote(ref, ref, ss.at[p, k], sr.at[p, k], sib)

    def own(p, go):
        @pl.when(z < last)
        def _():
            go(zcopy(p, 0, z))

        @pl.when(z > 0)
        def _():
            go(zcopy(p, 1, z))

        go(ycopy(p, z, y))

        @pl.when(z == 0)
        def _():
            go(zcopy(p, 0, z, last))

        @pl.when(z == last)
        def _():
            go(zcopy(p, 1, z, last))

        go(scopy(p, z * 2 + y, core))

    def near(t, fn):
        @pl.when(z >= t)
        def _():
            fn(0, z - t)

        @pl.when(z + t <= last)
        def _():
            fn(1, z + t)

    def forward(p, t, way, s, go):
        if t == 1:
            @pl.when(z < last if way == 0 else z > 0)
            def _():
                go(zcopy(p, way, s))
        go(ycopy(p, s, y))
        go(scopy(p, s * 2 + y, core))

    def hop(p, t):
        def arrive(way, s):
            zcopy(p, way, s).wait_recv()
            forward(p, t, way, s, lambda copy: copy.start())
        near(t, arrive)

    def across(p, t):
        def arrive(way, s):
            ycopy(p, s, 1 - y).wait_recv()
            scopy(p, s * 2 + 1 - y, core).start()
        if t == 0:
            arrive(0, z)
        else:
            near(t, arrive)

    def from_sibling(p, h):
        for k in range(4):
            scopy(p, 2 * base[h] + k, 1 - core).wait_recv()

    tile = 256
    tiles = hidden // tile

    def both(h, n):
        cols = slice(n * tile, (n + 1) * tile)
        stacked = xv[:, pl.ds(4 * base[h], 8)].reshape(2 * half, width)
        gate_both = jnp.dot(stacked, g[:, cols], preferred_element_type=F32)
        up_both = jnp.dot(stacked, u[:, cols], preferred_element_type=F32)
        gate, gate_dot = gate_both[:half], gate_both[half:]
        upper, up_dot = up_both[:half], up_both[half:]
        sigma = jax.nn.sigmoid(gate)
        first = sigma * (1.0 + gate * (1.0 - sigma))
        second = sigma * (1.0 - sigma) * (2.0 + gate * (1.0 - 2.0 * sigma))
        a_s[h, :, cols] = up_dot * first + upper * second * gate_dot
        b_s[h, :, cols] = first * gate_dot

    def changes(h):
        rows_c = cw[pl.ds(4 * base[h], 8)].reshape(half, width + LANES)
        tags = rows_c[:, width:].astype(F32)
        mine = lax.broadcasted_iota(jnp.int32, (half, LANES), 1) == me
        scale = jnp.sum(jnp.where(mine, tags, 0.0), axis=1, keepdims=True)
        for n in range(tiles):
            cols = slice(n * tile, (n + 1) * tile)
            back = lax.dot_general(
                rows_c[:, :width], d[cols, :], NT, preferred_element_type=F32
            )
            back = back * scale
            gc[h, :, cols] = (back * a_s[h, :, cols]).astype(BF16)
            uc[h, :, cols] = (back * b_s[h, :, cols]).astype(BF16)

    def to_sibling(h, j):
        return remote(s1.at[h, j], r1.at[h, j], sib_s.at[h, j], sib_r.at[h, j], sib)

    def to_column(h, j):
        return remote(s2.at[h, j], r2.at[h, j], col_s.at[h, j], col_r.at[h, j], ynb)

    def to_line(h, j, l):
        return remote(
            sq.at[h, j, l], rq.at[j, z], line_s.at[h, j, l], line_r.at[j, z],
            dev(base[h] + l, y, core),
        )

    def from_line(j, src):
        return remote(sq.at[1, j, 0], rq.at[j, src], line_s.at[1, j, 0], line_r.at[j, src], sib)

    def make_terms(h, j):
        cols = slice(j * piece, (j + 1) * piece)
        t = lax.dot_general(gc[h], g[cols, :], NT, preferred_element_type=F32)
        t = t + lax.dot_general(uc[h], u[cols, :], NT, preferred_element_type=F32)
        term[h, j] = t.reshape(8, rows, piece)
        for k in range(4):
            s1[h, j, k] = term[h, j, 2 * k + 1 - core].astype(BF16)
        to_sibling(h, j).start()

    def add_sibling(h, j):
        to_sibling(h, j).wait_recv()
        for l in range(2):
            s2[h, j, l] = (
                term[h, j, dev(l, 1 - y, core)] + r1[h, j, l * 2 + 1 - y].astype(F32)
            ).astype(BF16)
        to_column(h, j).start()
        for l in range(2):
            q[h, j, l] = term[h, j, dev(l, y, core)] + r1[h, j, l * 2 + y].astype(F32)

    def add_column(h, j):
        to_column(h, j).wait_recv()
        if h == 1:
            for l in range(2):
                sq[h, j, l] = (q[h, j, l] + r2[h, j, l].astype(F32)).astype(BF16)
                to_line(h, j, l).start()
        else:
            other = 1 - low
            sq[h, j, other] = (q[h, j, other] + r2[h, j, other].astype(F32)).astype(BF16)
            to_line(h, j, other).start()
            cols = slice(j * piece, (j + 1) * piece)
            out_ref[:, cols] = q[h, j, low] + r2[h, j, low].astype(F32)

    loads[0].wait()
    own(0, lambda copy: copy.start())
    loads[1].wait()
    own(1, lambda copy: copy.start())
    loads[2].wait()
    hop(0, 1)
    hop(1, 1)
    own(2, lambda copy: copy.start())
    across(0, 0)
    across(1, 0)
    hop(0, 2)
    hop(1, 2)
    hop(2, 1)
    across(0, 1)
    across(1, 1)
    across(2, 0)
    for load in loads[3:]:
        load.wait()
    from_sibling(0, 0)
    from_sibling(1, 0)
    hop(0, 3)
    hop(1, 3)
    both(0, 0)
    hop(2, 2)
    hop(2, 3)
    across(0, 2)
    across(1, 2)
    for n in range(1, tiles):
        both(0, n)
        across(n - 1, 3)
    across(2, 1)
    from_sibling(2, 0)
    changes(0)
    from_sibling(0, 1)
    from_sibling(1, 1)
    for n in range(tiles):
        both(1, n)
    across(2, 2)
    across(2, 3)
    for j in range(parts):
        make_terms(0, j)
    for j in range(parts):
        add_sibling(0, j)
    from_sibling(2, 1)
    changes(1)
    for j in range(parts):
        make_terms(1, j)
        if j > 0:
            add_sibling(1, j - 1)
    add_sibling(1, parts - 1)
    for j in range(parts):
        add_column(0, j)
    for j in range(parts):
        add_column(1, j)
    for j in range(parts):
        cols = slice(j * piece, (j + 1) * piece)
        sources = (base[0] + 1 - low, base[1], base[1] + 1)
        for src in sources:
            from_line(j, src).wait_recv()
        out_ref[:, cols] += (
            rq[j, sources[0]].astype(F32)
            + rq[j, sources[1]].astype(F32)
            + rq[j, sources[2]].astype(F32)
        )

    for p in range(3):
        own(p, lambda copy: copy.wait_send())
        scopy(p, z * 2 + 1 - y, core).wait_send()
        for t in range(1, lines):
            def gone(way, s):
                forward(p, t, way, s, lambda copy: copy.wait_send())
                scopy(p, s * 2 + 1 - y, core).wait_send()
            near(t, gone)
    for j in range(parts):
        for h in range(2):
            to_sibling(h, j).wait_send()
            to_column(h, j).wait_send()
        to_line(0, j, 1 - low).wait_send()
        to_line(1, j, 0).wait_send()
        to_line(1, j, 1).wait_send()


def whole_blocks(x, v, c, routes, rw, g, u, d):
    rows, width = x.shape
    hidden = g.shape[2]
    blocks = LINES * 4
    half = blocks * rows // 2
    parts = 2
    piece = width // parts
    dma = pltpu.SemaphoreType.DMA
    hbm = pl.BlockSpec(memory_space=pltpu.HBM)
    vmem = pl.BlockSpec(memory_space=pltpu.VMEM)
    return pl.pallas_call(
        whole_block_kernel,
        out_shape=jax.ShapeDtypeStruct((rows, width), F32),
        in_specs=[hbm] * 3 + [vmem] * 2 + [hbm] * 3,
        out_specs=vmem,
        scratch_shapes=[
            pltpu.VMEM((2, blocks, rows, width), BF16),
            pltpu.VMEM((blocks, rows, width + LANES), BF16),
            pltpu.VMEM((width, hidden), BF16),
            pltpu.VMEM((width, hidden), BF16),
            pltpu.VMEM((hidden, width), BF16),
            pltpu.VMEM((2, half, hidden), F32),
            pltpu.VMEM((2, half, hidden), F32),
            pltpu.VMEM((2, half, hidden), BF16),
            pltpu.VMEM((2, half, hidden), BF16),
            pltpu.VMEM((2, parts, blocks // 2, rows, piece), F32),
            pltpu.VMEM((2, parts, 2, rows, piece), F32),
            pltpu.VMEM((2, parts, 4, rows, piece), BF16),
            pltpu.VMEM((2, parts, 4, rows, piece), BF16),
            pltpu.VMEM((2, parts, 2, rows, piece), BF16),
            pltpu.VMEM((2, parts, 2, rows, piece), BF16),
            pltpu.VMEM((2, parts, 2, rows, piece), BF16),
            pltpu.VMEM((parts, LINES, rows, piece), BF16),
            dma((6,)),
            dma((3, 2, LINES, 2)),
            dma((3, 2, LINES)),
            dma((3, LINES)),
            dma((3, LINES)),
            dma((3, LINES * 2)),
            dma((3, LINES * 2)),
            dma((2, parts)),
            dma((2, parts)),
            dma((2, parts)),
            dma((2, parts)),
            dma((2, parts, 2)),
            dma((parts, LINES)),
        ],
        compiler_params=pltpu.CompilerParams(
            collective_id=0, has_side_effects=True, vmem_limit_bytes=56 * 2**20
        ),
        cost_estimate=pl.CostEstimate(
            flops=28 * half * width * hidden,
            bytes_accessed=6 * width * hidden + 10 * rows * width,
            transcendentals=2 * half * hidden,
        ),
    )(x, v, c, routes.T, rw.T, g, u, d)


def route_terms(rows_x, rows_v, rows_c, rows_w, gate_w, up_w, down_w):
    count = rows_x.shape[0]
    stacked = jnp.concatenate([rows_x, rows_v], axis=0)
    gate_both = jnp.dot(stacked, gate_w, preferred_element_type=jnp.float32)
    up_both = jnp.dot(stacked, up_w, preferred_element_type=jnp.float32)
    gate = gate_both[:count]
    gate_dot = gate_both[count:]
    upper = up_both[:count]
    up_dot = up_both[count:]
    back = lax.dot_general(
        rows_c, down_w, (((1,), (1,)), ((), ())), preferred_element_type=jnp.float32
    )
    back = back * rows_w.astype(jnp.float32)[:, None]
    sigma = jax.nn.sigmoid(gate)
    first = sigma * (1.0 + gate * (1.0 - sigma))
    second = sigma * (1.0 - sigma) * (2.0 + gate * (1.0 - 2.0 * sigma))
    gate_change = (back * (up_dot * first + upper * second * gate_dot)).astype(jnp.bfloat16)
    up_change = (back * first * gate_dot).astype(jnp.bfloat16)
    term = lax.dot_general(
        gate_change, gate_w, (((1,), (1,)), ((), ())), preferred_element_type=jnp.float32
    )
    term = term + lax.dot_general(
        up_change, up_w, (((1,), (1,)), ((), ())), preferred_element_type=jnp.float32
    )
    return term.astype(jnp.bfloat16)


def shards(tokens, tangent, cotangent, routes, route_weight, gate_weight, up_weight, down_weight):
    experts = lax.axis_size("expert")
    tok_rows, width = tokens.shape
    top_count = routes.shape[1]
    slots = 2 * tok_rows * top_count // experts
    if slots >= tok_rows and experts == 4 * LINES:
        return whole_blocks(
            tokens, tangent, cotangent, routes, route_weight, gate_weight, up_weight, down_weight
        )
    routed = tok_rows * top_count
    flat_routes = routes.reshape(-1)
    onehot = (flat_routes[:, None] == jnp.arange(experts, dtype=jnp.int32)[None, :]).astype(
        jnp.int32
    )
    slot_rank = jnp.sum((jnp.cumsum(onehot, axis=0) - onehot) * onehot, axis=1)
    target = flat_routes * slots + slot_rank
    source = (
        jnp.zeros((experts * slots,), jnp.int32).at[target].set(jnp.arange(routed, dtype=jnp.int32))
    )
    filled = jnp.zeros((experts * slots,), jnp.bool_).at[target].set(True)
    owner = source // top_count

    def place(values):
        picked = jnp.where(filled[:, None], values[owner], jnp.zeros((), values.dtype))
        return picked.reshape(experts, slots, width)

    send_x = place(tokens)
    send_v = place(tangent)
    send_c = place(cotangent)
    send_w = jnp.where(
        filled, route_weight.reshape(-1)[source], jnp.zeros((), route_weight.dtype)
    ).reshape(experts, slots)
    gate_w = gate_weight[0]
    up_w = up_weight[0]
    down_w = down_weight[0]
    recv_w = lax.all_to_all(send_w, "expert", split_axis=0, concat_axis=0, tiled=True)
    sources, levels = recv_w.shape
    result = route_terms(
        lax.all_to_all(send_x, "expert", split_axis=0, concat_axis=0, tiled=True).reshape(
            -1, width
        ),
        lax.all_to_all(send_v, "expert", split_axis=0, concat_axis=0, tiled=True).reshape(
            -1, width
        ),
        lax.all_to_all(send_c, "expert", split_axis=0, concat_axis=0, tiled=True).reshape(
            -1, width
        ),
        recv_w.reshape(-1),
        gate_w,
        up_w,
        down_w,
    )
    terms = result.reshape(sources, levels, width)
    returned = lax.all_to_all(terms, "expert", split_axis=0, concat_axis=0, tiled=True)
    back_flat = returned.reshape(experts * slots, width)
    per_route = back_flat[target].astype(jnp.float32).reshape(tok_rows, top_count, width)
    return jnp.sum(per_route, axis=1)


def solution(mesh):
    placed = (
        P(("groups", "expert"), None),
        P(("groups", "expert"), None),
        P(("groups", "expert"), None),
        P(("groups", "expert"), None),
        P(("groups", "expert"), None),
        P("expert", None, None),
        P("expert", None, None),
        P("expert", None, None),
    )
    return jax.shard_map(
        shards, mesh=mesh, in_specs=placed, out_specs=P(("groups", "expert"), None), check_vma=False
    )
```

```python
import jax
import jax.numpy as jnp
from jax import lax
from jax.experimental import pallas as pl
from jax.experimental.pallas import tpu as pltpu
from jax.sharding import PartitionSpec as P

LANES = 128
LINES = 4
BF16 = jnp.bfloat16
F32 = jnp.float32
NT = (((1,), (1,)), ((), ()))


def whole_block_kernel(
    x_hbm, v_hbm, c_hbm, routes_ref, rw_ref, g_hbm, u_hbm, d_hbm, out_ref,
    xv, cw, g, u, d, a_s, b_s, gc, uc, term, q,
    s1, r1, s2, r2, sq, rq,
    local, zs, zr, ys, yr, ss, sr, sib_s, sib_r, col_s, col_r, line_s, line_r,
):
    rows, width = x_hbm.shape
    hidden = g.shape[1]
    lines = LINES
    last = lines - 1
    half = lines * 2 * rows
    parts = term.shape[1]
    piece = width // parts
    me = lax.axis_index("expert")
    core = lax.rem(me, 2)
    y = lax.rem(lax.div(me, 2), 2)
    z = lax.div(me, 4)
    pair = lax.div(z, 2)
    low = lax.rem(z, 2)
    base = (2 * pair, 2 * (1 - pair))

    def dev(zz, yy, cc):
        return (zz * 2 + yy) * 2 + cc

    sib = dev(z, y, 1 - core)
    ynb = dev(z, 1 - y, core)

    def remote(src, dst, send, recv, target):
        return pltpu.make_async_remote_copy(
            src_ref=src, dst_ref=dst, send_sem=send, recv_sem=recv,
            device_id={"expert": target}, device_id_type=pl.DeviceIdType.MESH,
        )

    loads = [
        pltpu.make_async_copy(x_hbm, xv.at[0, me], local.at[0]),
        pltpu.make_async_copy(v_hbm, xv.at[1, me], local.at[1]),
        pltpu.make_async_copy(c_hbm, cw.at[me, :, pl.ds(0, width)], local.at[2]),
        pltpu.make_async_copy(g_hbm.at[0], g, local.at[3]),
        pltpu.make_async_copy(u_hbm.at[0], u, local.at[4]),
        pltpu.make_async_copy(d_hbm.at[0], d, local.at[5]),
    ]
    for load in loads:
        load.start()

    barrier = pltpu.get_barrier_semaphore()

    def greet(target):
        pl.semaphore_signal(
            barrier, inc=1, device_id={"expert": target}, device_id_type=pl.DeviceIdType.MESH
        )

    greet(sib)
    greet(ynb)

    @pl.when(z > 0)
    def _():
        greet(me - 4)

    @pl.when(z < last)
    def _():
        greet(me + 4)

    lane = lax.broadcasted_iota(jnp.int32, (rows, LANES), 1)
    eye = lax.broadcasted_iota(jnp.int32, (rows, rows), 0) == lax.broadcasted_iota(
        jnp.int32, (rows, rows), 1
    )
    routes = routes_ref[...].astype(F32)
    weights = rw_ref[...].astype(F32)
    table = jnp.zeros((rows, LANES), F32)
    for k in range(routes.shape[0]):
        route = jnp.sum(jnp.where(eye, routes[k : k + 1, :], 0.0), axis=1, keepdims=True)
        weight = jnp.sum(jnp.where(eye, weights[k : k + 1, :], 0.0), axis=1, keepdims=True)
        table = table + jnp.where(route.astype(jnp.int32) == lane, weight, 0.0)
    cw[me, :, width:] = table.astype(BF16)

    pl.semaphore_wait(barrier, 2 + (z > 0).astype(jnp.int32) + (z < last).astype(jnp.int32))

    def block(p, index):
        return cw.at[index] if p == 2 else xv.at[p, index]

    def zcopy(p, way, s):
        ref = block(p, dev(s, y, core))
        target = me + 4 if way == 0 else me - 4
        return remote(ref, ref, zs.at[p, way, s], zr.at[p, way, s], target)

    def ycopy(p, s, col):
        ref = block(p, dev(s, col, core))
        return remote(ref, ref, ys.at[p, s], yr.at[p, s], ynb)

    def scopy(p, k, plane):
        ref = block(p, k * 2 + plane)
        return remote(ref, ref, ss.at[p, k], sr.at[p, k], sib)

    def own(p, go):
        @pl.when(z < last)
        def _():
            go(zcopy(p, 0, z))

        @pl.when(z > 0)
        def _():
            go(zcopy(p, 1, z))

        go(ycopy(p, z, y))

        go(scopy(p, z * 2 + y, core))

    def near(t, fn):
        @pl.when(z >= t)
        def _():
            fn(0, z - t)

        @pl.when(z + t <= last)
        def _():
            fn(1, z + t)

    def forward(p, t, way, s, go):
        @pl.when(z < last if way == 0 else z > 0)
        def _():
            go(zcopy(p, way, s))

        go(ycopy(p, s, y))
        go(scopy(p, s * 2 + y, core))

    def hop(p, t):
        def arrive(way, s):
            zcopy(p, way, s).wait_recv()
            forward(p, t, way, s, lambda copy: copy.start())
        near(t, arrive)

    def across(p, t):
        def arrive(way, s):
            ycopy(p, s, 1 - y).wait_recv()
            scopy(p, s * 2 + 1 - y, core).start()
        if t == 0:
            arrive(0, z)
        else:
            near(t, arrive)

    def from_sibling(p, h):
        for k in range(4):
            scopy(p, 2 * base[h] + k, 1 - core).wait_recv()

    tile = 256
    tiles = hidden // tile

    def both(h, n):
        cols = slice(n * tile, (n + 1) * tile)
        stacked = xv[:, pl.ds(4 * base[h], 8)].reshape(2 * half, width)
        gate_both = jnp.dot(stacked, g[:, cols], preferred_element_type=F32)
        up_both = jnp.dot(stacked, u[:, cols], preferred_element_type=F32)
        gate, gate_dot = gate_both[:half], gate_both[half:]
        upper, up_dot = up_both[:half], up_both[half:]
        sigma = jax.nn.sigmoid(gate)
        first = sigma * (1.0 + gate * (1.0 - sigma))
        second = sigma * (1.0 - sigma) * (2.0 + gate * (1.0 - 2.0 * sigma))
        a_s[h, :, cols] = up_dot * first + upper * second * gate_dot
        b_s[h, :, cols] = first * gate_dot

    def changes(h):
        rows_c = cw[pl.ds(4 * base[h], 8)].reshape(half, width + LANES)
        tags = rows_c[:, width:].astype(F32)
        mine = lax.broadcasted_iota(jnp.int32, (half, LANES), 1) == me
        scale = jnp.sum(jnp.where(mine, tags, 0.0), axis=1, keepdims=True)
        for n in range(tiles):
            cols = slice(n * tile, (n + 1) * tile)
            back = lax.dot_general(
                rows_c[:, :width], d[cols, :], NT, preferred_element_type=F32
            )
            back = back * scale
            gc[h, :, cols] = (back * a_s[h, :, cols]).astype(BF16)
            uc[h, :, cols] = (back * b_s[h, :, cols]).astype(BF16)

    def to_sibling(h, j):
        return remote(s1.at[h, j], r1.at[h, j], sib_s.at[h, j], sib_r.at[h, j], sib)

    def to_column(h, j):
        return remote(s2.at[h, j], r2.at[h, j], col_s.at[h, j], col_r.at[h, j], ynb)

    def to_line(h, j, l):
        return remote(
            sq.at[h, j, l], rq.at[j, z], line_s.at[h, j, l], line_r.at[j, z],
            dev(base[h] + l, y, core),
        )

    def from_line(j, src):
        return remote(sq.at[1, j, 0], rq.at[j, src], line_s.at[1, j, 0], line_r.at[j, src], sib)

    def make_terms(h, j):
        cols = slice(j * piece, (j + 1) * piece)
        t = lax.dot_general(gc[h], g[cols, :], NT, preferred_element_type=F32)
        t = t + lax.dot_general(uc[h], u[cols, :], NT, preferred_element_type=F32)
        term[h, j] = t.reshape(8, rows, piece)
        for k in range(4):
            s1[h, j, k] = term[h, j, 2 * k + 1 - core].astype(BF16)
        to_sibling(h, j).start()

    def add_sibling(h, j):
        to_sibling(h, j).wait_recv()
        for l in range(2):
            s2[h, j, l] = (
                term[h, j, dev(l, 1 - y, core)] + r1[h, j, l * 2 + 1 - y].astype(F32)
            ).astype(BF16)
        to_column(h, j).start()
        for l in range(2):
            q[h, j, l] = term[h, j, dev(l, y, core)] + r1[h, j, l * 2 + y].astype(F32)

    def add_column(h, j):
        to_column(h, j).wait_recv()
        if h == 1:
            for l in range(2):
                sq[h, j, l] = (q[h, j, l] + r2[h, j, l].astype(F32)).astype(BF16)
                to_line(h, j, l).start()
        else:
            other = 1 - low
            sq[h, j, other] = (q[h, j, other] + r2[h, j, other].astype(F32)).astype(BF16)
            to_line(h, j, other).start()
            cols = slice(j * piece, (j + 1) * piece)
            out_ref[:, cols] = q[h, j, low] + r2[h, j, low].astype(F32)

    loads[0].wait()
    own(0, lambda copy: copy.start())
    loads[1].wait()
    own(1, lambda copy: copy.start())
    loads[2].wait()
    hop(0, 1)
    hop(1, 1)
    own(2, lambda copy: copy.start())
    across(0, 0)
    across(1, 0)
    hop(0, 2)
    hop(1, 2)
    hop(2, 1)
    across(0, 1)
    across(1, 1)
    for load in loads[3:]:
        load.wait()
    from_sibling(0, 0)
    from_sibling(1, 0)
    both(0, 0)
    hop(0, 3)
    both(0, 1)
    hop(1, 3)
    hop(2, 2)
    across(2, 0)
    across(0, 2)
    both(0, 2)
    across(1, 2)
    across(2, 1)
    from_sibling(2, 0)
    changes(0)
    across(0, 3)
    hop(2, 3)
    for j in range(parts):
        make_terms(0, j)
    across(1, 3)
    from_sibling(0, 1)
    from_sibling(1, 1)
    both(1, 0)
    for j in range(parts):
        add_sibling(0, j)
    both(1, 1)
    across(2, 2)
    both(1, 2)
    across(2, 3)
    from_sibling(2, 1)
    changes(1)
    for j in range(parts):
        make_terms(1, j)
        if j > 0:
            add_sibling(1, j - 1)
    add_sibling(1, parts - 1)
    for j in range(parts):
        add_column(0, j)
    for j in range(parts):
        add_column(1, j)
    for j in range(parts):
        cols = slice(j * piece, (j + 1) * piece)
        sources = (base[0] + 1 - low, base[1], base[1] + 1)
        for src in sources:
            from_line(j, src).wait_recv()
        out_ref[:, cols] += (
            rq[j, sources[0]].astype(F32)
            + rq[j, sources[1]].astype(F32)
            + rq[j, sources[2]].astype(F32)
        )

    for p in range(3):
        own(p, lambda copy: copy.wait_send())
        scopy(p, z * 2 + 1 - y, core).wait_send()
        for t in range(1, lines):
            def gone(way, s):
                forward(p, t, way, s, lambda copy: copy.wait_send())
                scopy(p, s * 2 + 1 - y, core).wait_send()
            near(t, gone)
    for j in range(parts):
        for h in range(2):
            to_sibling(h, j).wait_send()
            to_column(h, j).wait_send()
        to_line(0, j, 1 - low).wait_send()
        to_line(1, j, 0).wait_send()
        to_line(1, j, 1).wait_send()


def whole_blocks(x, v, c, routes, rw, g, u, d):
    rows, width = x.shape
    hidden = g.shape[2]
    blocks = LINES * 4
    half = blocks * rows // 2
    parts = 2
    piece = width // parts
    dma = pltpu.SemaphoreType.DMA
    hbm = pl.BlockSpec(memory_space=pltpu.HBM)
    vmem = pl.BlockSpec(memory_space=pltpu.VMEM)
    return pl.pallas_call(
        whole_block_kernel,
        out_shape=jax.ShapeDtypeStruct((rows, width), F32),
        in_specs=[hbm] * 3 + [vmem] * 2 + [hbm] * 3,
        out_specs=vmem,
        scratch_shapes=[
            pltpu.VMEM((2, blocks, rows, width), BF16),
            pltpu.VMEM((blocks, rows, width + LANES), BF16),
            pltpu.VMEM((width, hidden), BF16),
            pltpu.VMEM((width, hidden), BF16),
            pltpu.VMEM((hidden, width), BF16),
            pltpu.VMEM((2, half, hidden), F32),
            pltpu.VMEM((2, half, hidden), F32),
            pltpu.VMEM((2, half, hidden), BF16),
            pltpu.VMEM((2, half, hidden), BF16),
            pltpu.VMEM((2, parts, blocks // 2, rows, piece), F32),
            pltpu.VMEM((2, parts, 2, rows, piece), F32),
            pltpu.VMEM((2, parts, 4, rows, piece), BF16),
            pltpu.VMEM((2, parts, 4, rows, piece), BF16),
            pltpu.VMEM((2, parts, 2, rows, piece), BF16),
            pltpu.VMEM((2, parts, 2, rows, piece), BF16),
            pltpu.VMEM((2, parts, 2, rows, piece), BF16),
            pltpu.VMEM((parts, LINES, rows, piece), BF16),
            dma((6,)),
            dma((3, 2, LINES)),
            dma((3, 2, LINES)),
            dma((3, LINES)),
            dma((3, LINES)),
            dma((3, LINES * 2)),
            dma((3, LINES * 2)),
            dma((2, parts)),
            dma((2, parts)),
            dma((2, parts)),
            dma((2, parts)),
            dma((2, parts, 2)),
            dma((parts, LINES)),
        ],
        compiler_params=pltpu.CompilerParams(
            collective_id=0, has_side_effects=True, vmem_limit_bytes=56 * 2**20
        ),
        cost_estimate=pl.CostEstimate(
            flops=28 * half * width * hidden,
            bytes_accessed=6 * width * hidden + 10 * rows * width,
            transcendentals=2 * half * hidden,
        ),
    )(x, v, c, routes.T, rw.T, g, u, d)


def route_terms(rows_x, rows_v, rows_c, rows_w, gate_w, up_w, down_w):
    count = rows_x.shape[0]
    stacked = jnp.concatenate([rows_x, rows_v], axis=0)
    gate_both = jnp.dot(stacked, gate_w, preferred_element_type=jnp.float32)
    up_both = jnp.dot(stacked, up_w, preferred_element_type=jnp.float32)
    gate = gate_both[:count]
    gate_dot = gate_both[count:]
    upper = up_both[:count]
    up_dot = up_both[count:]
    back = lax.dot_general(
        rows_c, down_w, (((1,), (1,)), ((), ())), preferred_element_type=jnp.float32
    )
    back = back * rows_w.astype(jnp.float32)[:, None]
    sigma = jax.nn.sigmoid(gate)
    first = sigma * (1.0 + gate * (1.0 - sigma))
    second = sigma * (1.0 - sigma) * (2.0 + gate * (1.0 - 2.0 * sigma))
    gate_change = (back * (up_dot * first + upper * second * gate_dot)).astype(jnp.bfloat16)
    up_change = (back * first * gate_dot).astype(jnp.bfloat16)
    term = lax.dot_general(
        gate_change, gate_w, (((1,), (1,)), ((), ())), preferred_element_type=jnp.float32
    )
    term = term + lax.dot_general(
        up_change, up_w, (((1,), (1,)), ((), ())), preferred_element_type=jnp.float32
    )
    return term.astype(jnp.bfloat16)


def shards(tokens, tangent, cotangent, routes, route_weight, gate_weight, up_weight, down_weight):
    experts = lax.axis_size("expert")
    tok_rows, width = tokens.shape
    top_count = routes.shape[1]
    slots = 2 * tok_rows * top_count // experts
    if slots >= tok_rows and experts == 4 * LINES:
        return whole_blocks(
            tokens, tangent, cotangent, routes, route_weight, gate_weight, up_weight, down_weight
        )
    routed = tok_rows * top_count
    flat_routes = routes.reshape(-1)
    onehot = (flat_routes[:, None] == jnp.arange(experts, dtype=jnp.int32)[None, :]).astype(
        jnp.int32
    )
    slot_rank = jnp.sum((jnp.cumsum(onehot, axis=0) - onehot) * onehot, axis=1)
    target = flat_routes * slots + slot_rank
    source = (
        jnp.zeros((experts * slots,), jnp.int32).at[target].set(jnp.arange(routed, dtype=jnp.int32))
    )
    filled = jnp.zeros((experts * slots,), jnp.bool_).at[target].set(True)
    owner = source // top_count

    def place(values):
        picked = jnp.where(filled[:, None], values[owner], jnp.zeros((), values.dtype))
        return picked.reshape(experts, slots, width)

    send_x = place(tokens)
    send_v = place(tangent)
    send_c = place(cotangent)
    send_w = jnp.where(
        filled, route_weight.reshape(-1)[source], jnp.zeros((), route_weight.dtype)
    ).reshape(experts, slots)
    gate_w = gate_weight[0]
    up_w = up_weight[0]
    down_w = down_weight[0]
    recv_w = lax.all_to_all(send_w, "expert", split_axis=0, concat_axis=0, tiled=True)
    sources, levels = recv_w.shape
    result = route_terms(
        lax.all_to_all(send_x, "expert", split_axis=0, concat_axis=0, tiled=True).reshape(
            -1, width
        ),
        lax.all_to_all(send_v, "expert", split_axis=0, concat_axis=0, tiled=True).reshape(
            -1, width
        ),
        lax.all_to_all(send_c, "expert", split_axis=0, concat_axis=0, tiled=True).reshape(
            -1, width
        ),
        recv_w.reshape(-1),
        gate_w,
        up_w,
        down_w,
    )
    terms = result.reshape(sources, levels, width)
    returned = lax.all_to_all(terms, "expert", split_axis=0, concat_axis=0, tiled=True)
    back_flat = returned.reshape(experts * slots, width)
    per_route = back_flat[target].astype(jnp.float32).reshape(tok_rows, top_count, width)
    return jnp.sum(per_route, axis=1)


def solution(mesh):
    placed = (
        P(("groups", "expert"), None),
        P(("groups", "expert"), None),
        P(("groups", "expert"), None),
        P(("groups", "expert"), None),
        P(("groups", "expert"), None),
        P("expert", None, None),
        P("expert", None, None),
        P("expert", None, None),
    )
    return jax.shard_map(
        shards, mesh=mesh, in_specs=placed, out_specs=P(("groups", "expert"), None), check_vma=False
    )
```

```python
import jax
import jax.numpy as jnp
from jax import lax
from jax.experimental import pallas as pl
from jax.experimental.pallas import tpu as pltpu
from jax.sharding import PartitionSpec as P

LANES = 128
LINES = 4
BF16 = jnp.bfloat16
F32 = jnp.float32
NT = (((1,), (1,)), ((), ()))


def whole_block_kernel(
    x_hbm, v_hbm, c_hbm, routes_ref, rw_ref, g_hbm, u_hbm, d_hbm, out_ref,
    xv, cw, g, u, d, a_s, b_s, gc, uc, term, q,
    s1, r1, s2, r2, sq, rq,
    local, zs, zr, ys, yr, ss, sr, sib_s, sib_r, col_s, col_r, line_s, line_r,
):
    rows, width = x_hbm.shape
    hidden = g.shape[1]
    lines = LINES
    last = lines - 1
    half = lines * 2 * rows
    parts = term.shape[1]
    piece = width // parts
    me = lax.axis_index("expert")
    core = lax.rem(me, 2)
    y = lax.rem(lax.div(me, 2), 2)
    z = lax.div(me, 4)
    pair = lax.div(z, 2)
    low = lax.rem(z, 2)
    base = (2 * pair, 2 * (1 - pair))

    def dev(zz, yy, cc):
        return (zz * 2 + yy) * 2 + cc

    sib = dev(z, y, 1 - core)
    ynb = dev(z, 1 - y, core)

    def remote(src, dst, send, recv, target):
        return pltpu.make_async_remote_copy(
            src_ref=src, dst_ref=dst, send_sem=send, recv_sem=recv,
            device_id={"expert": target}, device_id_type=pl.DeviceIdType.MESH,
        )

    loads = [
        pltpu.make_async_copy(x_hbm, xv.at[0, me], local.at[0]),
        pltpu.make_async_copy(v_hbm, xv.at[1, me], local.at[1]),
        pltpu.make_async_copy(c_hbm, cw.at[me, :, pl.ds(0, width)], local.at[2]),
        pltpu.make_async_copy(g_hbm.at[0], g, local.at[3]),
        pltpu.make_async_copy(u_hbm.at[0], u, local.at[4]),
        pltpu.make_async_copy(d_hbm.at[0], d, local.at[5]),
    ]
    for load in loads:
        load.start()

    barrier = pltpu.get_barrier_semaphore()

    def greet(target):
        pl.semaphore_signal(
            barrier, inc=1, device_id={"expert": target}, device_id_type=pl.DeviceIdType.MESH
        )

    greet(sib)
    greet(ynb)

    @pl.when(z > 0)
    def _():
        greet(me - 4)

    @pl.when(z < last)
    def _():
        greet(me + 4)

    pl.semaphore_wait(barrier, 2 + (z > 0).astype(jnp.int32) + (z < last).astype(jnp.int32))

    def block(p, index):
        return cw.at[index] if p == 2 else xv.at[p, index]

    def zcopy(p, way, s):
        ref = block(p, dev(s, y, core))
        target = me + 4 if way == 0 else me - 4
        return remote(ref, ref, zs.at[p, way, s], zr.at[p, way, s], target)

    def ycopy(p, s, col):
        ref = block(p, dev(s, col, core))
        return remote(ref, ref, ys.at[p, s], yr.at[p, s], ynb)

    def scopy(p, k, plane):
        ref = block(p, k * 2 + plane)
        return remote(ref, ref, ss.at[p, k], sr.at[p, k], sib)

    def own(p, go):
        @pl.when(z < last)
        def _():
            go(zcopy(p, 0, z))

        @pl.when(z > 0)
        def _():
            go(zcopy(p, 1, z))

        go(ycopy(p, z, y))

        go(scopy(p, z * 2 + y, core))

    def near(t, fn):
        @pl.when(z >= t)
        def _():
            fn(0, z - t)

        @pl.when(z + t <= last)
        def _():
            fn(1, z + t)

    def forward(p, t, way, s, go):
        @pl.when(z < last if way == 0 else z > 0)
        def _():
            go(zcopy(p, way, s))

        go(ycopy(p, s, y))
        go(scopy(p, s * 2 + y, core))

    def hop(p, t):
        def arrive(way, s):
            zcopy(p, way, s).wait_recv()
            forward(p, t, way, s, lambda copy: copy.start())
        near(t, arrive)

    def across(p, t):
        def arrive(way, s):
            ycopy(p, s, 1 - y).wait_recv()
            scopy(p, s * 2 + 1 - y, core).start()
        if t == 0:
            arrive(0, z)
        else:
            near(t, arrive)

    def from_sibling(p, h):
        for k in range(4):
            scopy(p, 2 * base[h] + k, 1 - core).wait_recv()

    tile = 256
    tiles = hidden // tile

    def both(h, n):
        cols = slice(n * tile, (n + 1) * tile)
        stacked = xv[:, pl.ds(4 * base[h], 8)].reshape(2 * half, width)
        gate_both = jnp.dot(stacked, g[:, cols], preferred_element_type=F32)
        up_both = jnp.dot(stacked, u[:, cols], preferred_element_type=F32)
        gate, gate_dot = gate_both[:half], gate_both[half:]
        upper, up_dot = up_both[:half], up_both[half:]
        sigma = jax.nn.sigmoid(gate)
        first = sigma * (1.0 + gate * (1.0 - sigma))
        second = sigma * (1.0 - sigma) * (2.0 + gate * (1.0 - 2.0 * sigma))
        a_s[h, :, cols] = up_dot * first + upper * second * gate_dot
        b_s[h, :, cols] = first * gate_dot

    def changes(h):
        rows_c = cw[pl.ds(4 * base[h], 8)].reshape(half, width + LANES)
        tags = rows_c[:, width:].astype(F32)
        mine = lax.broadcasted_iota(jnp.int32, (half, LANES), 1) == me
        scale = jnp.sum(jnp.where(mine, tags, 0.0), axis=1, keepdims=True)
        for n in range(tiles):
            cols = slice(n * tile, (n + 1) * tile)
            back = lax.dot_general(
                rows_c[:, :width], d[cols, :], NT, preferred_element_type=F32
            )
            back = back * scale
            gc[h, :, cols] = (back * a_s[h, :, cols]).astype(BF16)
            uc[h, :, cols] = (back * b_s[h, :, cols]).astype(BF16)

    def to_sibling(h, j):
        return remote(s1.at[h, j], r1.at[h, j], sib_s.at[h, j], sib_r.at[h, j], sib)

    def to_column(h, j):
        return remote(s2.at[h, j], r2.at[h, j], col_s.at[h, j], col_r.at[h, j], ynb)

    def to_line(h, j, l):
        return remote(
            sq.at[h, j, l], rq.at[j, z], line_s.at[h, j, l], line_r.at[j, z],
            dev(base[h] + l, y, core),
        )

    def from_line(j, src):
        return remote(sq.at[1, j, 0], rq.at[j, src], line_s.at[1, j, 0], line_r.at[j, src], sib)

    def make_terms(h, j):
        cols = slice(j * piece, (j + 1) * piece)
        t = lax.dot_general(gc[h], g[cols, :], NT, preferred_element_type=F32)
        t = t + lax.dot_general(uc[h], u[cols, :], NT, preferred_element_type=F32)
        term[h, j] = t.reshape(8, rows, piece)
        for k in range(4):
            s1[h, j, k] = term[h, j, 2 * k + 1 - core].astype(BF16)
        to_sibling(h, j).start()

    def add_sibling(h, j):
        to_sibling(h, j).wait_recv()
        for l in range(2):
            s2[h, j, l] = (
                term[h, j, dev(l, 1 - y, core)] + r1[h, j, l * 2 + 1 - y].astype(F32)
            ).astype(BF16)
        to_column(h, j).start()
        for l in range(2):
            q[h, j, l] = term[h, j, dev(l, y, core)] + r1[h, j, l * 2 + y].astype(F32)

    def add_column(h, j):
        to_column(h, j).wait_recv()
        if h == 1:
            for l in range(2):
                sq[h, j, l] = (q[h, j, l] + r2[h, j, l].astype(F32)).astype(BF16)
                to_line(h, j, l).start()
        else:
            other = 1 - low
            sq[h, j, other] = (q[h, j, other] + r2[h, j, other].astype(F32)).astype(BF16)
            to_line(h, j, other).start()
            cols = slice(j * piece, (j + 1) * piece)
            out_ref[:, cols] = q[h, j, low] + r2[h, j, low].astype(F32)

    loads[0].wait()
    own(0, lambda copy: copy.start())
    loads[1].wait()
    own(1, lambda copy: copy.start())
    lane = lax.broadcasted_iota(jnp.int32, (rows, LANES), 1)
    eye = lax.broadcasted_iota(jnp.int32, (rows, rows), 0) == lax.broadcasted_iota(
        jnp.int32, (rows, rows), 1
    )
    routes = routes_ref[...].astype(F32)
    weights = rw_ref[...].astype(F32)
    table = jnp.zeros((rows, LANES), F32)
    for k in range(routes.shape[0]):
        route = jnp.sum(jnp.where(eye, routes[k : k + 1, :], 0.0), axis=1, keepdims=True)
        weight = jnp.sum(jnp.where(eye, weights[k : k + 1, :], 0.0), axis=1, keepdims=True)
        table = table + jnp.where(route.astype(jnp.int32) == lane, weight, 0.0)
    cw[me, :, width:] = table.astype(BF16)

    loads[2].wait()
    hop(0, 1)
    hop(1, 1)
    own(2, lambda copy: copy.start())
    across(0, 0)
    across(1, 0)
    hop(0, 2)
    hop(1, 2)
    hop(2, 1)
    across(0, 1)
    across(1, 1)
    for load in loads[3:]:
        load.wait()
    from_sibling(0, 0)
    from_sibling(1, 0)
    both(0, 0)
    hop(0, 3)
    both(0, 1)
    hop(1, 3)
    hop(2, 2)
    across(2, 0)
    across(0, 2)
    both(0, 2)
    across(1, 2)
    across(2, 1)
    from_sibling(2, 0)
    changes(0)
    across(0, 3)
    hop(2, 3)
    for j in range(parts):
        make_terms(0, j)
    across(1, 3)
    from_sibling(0, 1)
    from_sibling(1, 1)
    both(1, 0)
    for j in range(parts):
        add_sibling(0, j)
    both(1, 1)
    across(2, 2)
    both(1, 2)
    across(2, 3)
    from_sibling(2, 1)
    changes(1)
    for j in range(parts):
        make_terms(1, j)
        if j > 0:
            add_sibling(1, j - 1)
    add_sibling(1, parts - 1)
    for j in range(parts):
        add_column(0, j)
    for j in range(parts):
        add_column(1, j)
    for j in range(parts):
        cols = slice(j * piece, (j + 1) * piece)
        sources = (base[0] + 1 - low, base[1], base[1] + 1)
        for src in sources:
            from_line(j, src).wait_recv()
        out_ref[:, cols] += (
            rq[j, sources[0]].astype(F32)
            + rq[j, sources[1]].astype(F32)
            + rq[j, sources[2]].astype(F32)
        )

    for p in range(3):
        own(p, lambda copy: copy.wait_send())
        scopy(p, z * 2 + 1 - y, core).wait_send()
        for t in range(1, lines):
            def gone(way, s):
                forward(p, t, way, s, lambda copy: copy.wait_send())
                scopy(p, s * 2 + 1 - y, core).wait_send()
            near(t, gone)
    for j in range(parts):
        for h in range(2):
            to_sibling(h, j).wait_send()
            to_column(h, j).wait_send()
        to_line(0, j, 1 - low).wait_send()
        to_line(1, j, 0).wait_send()
        to_line(1, j, 1).wait_send()


def whole_blocks(x, v, c, routes, rw, g, u, d):
    rows, width = x.shape
    hidden = g.shape[2]
    blocks = LINES * 4
    half = blocks * rows // 2
    parts = 2
    piece = width // parts
    dma = pltpu.SemaphoreType.DMA
    hbm = pl.BlockSpec(memory_space=pltpu.HBM)
    vmem = pl.BlockSpec(memory_space=pltpu.VMEM)
    return pl.pallas_call(
        whole_block_kernel,
        out_shape=jax.ShapeDtypeStruct((rows, width), F32),
        in_specs=[hbm] * 3 + [vmem] * 2 + [hbm] * 3,
        out_specs=vmem,
        scratch_shapes=[
            pltpu.VMEM((2, blocks, rows, width), BF16),
            pltpu.VMEM((blocks, rows, width + LANES), BF16),
            pltpu.VMEM((width, hidden), BF16),
            pltpu.VMEM((width, hidden), BF16),
            pltpu.VMEM((hidden, width), BF16),
            pltpu.VMEM((2, half, hidden), F32),
            pltpu.VMEM((2, half, hidden), F32),
            pltpu.VMEM((2, half, hidden), BF16),
            pltpu.VMEM((2, half, hidden), BF16),
            pltpu.VMEM((2, parts, blocks // 2, rows, piece), F32),
            pltpu.VMEM((2, parts, 2, rows, piece), F32),
            pltpu.VMEM((2, parts, 4, rows, piece), BF16),
            pltpu.VMEM((2, parts, 4, rows, piece), BF16),
            pltpu.VMEM((2, parts, 2, rows, piece), BF16),
            pltpu.VMEM((2, parts, 2, rows, piece), BF16),
            pltpu.VMEM((2, parts, 2, rows, piece), BF16),
            pltpu.VMEM((parts, LINES, rows, piece), BF16),
            dma((6,)),
            dma((3, 2, LINES)),
            dma((3, 2, LINES)),
            dma((3, LINES)),
            dma((3, LINES)),
            dma((3, LINES * 2)),
            dma((3, LINES * 2)),
            dma((2, parts)),
            dma((2, parts)),
            dma((2, parts)),
            dma((2, parts)),
            dma((2, parts, 2)),
            dma((parts, LINES)),
        ],
        compiler_params=pltpu.CompilerParams(
            collective_id=0, has_side_effects=True, vmem_limit_bytes=56 * 2**20
        ),
        cost_estimate=pl.CostEstimate(
            flops=28 * half * width * hidden,
            bytes_accessed=6 * width * hidden + 10 * rows * width,
            transcendentals=2 * half * hidden,
        ),
    )(x, v, c, routes.T, rw.T, g, u, d)


def route_terms(rows_x, rows_v, rows_c, rows_w, gate_w, up_w, down_w):
    count = rows_x.shape[0]
    stacked = jnp.concatenate([rows_x, rows_v], axis=0)
    gate_both = jnp.dot(stacked, gate_w, preferred_element_type=jnp.float32)
    up_both = jnp.dot(stacked, up_w, preferred_element_type=jnp.float32)
    gate = gate_both[:count]
    gate_dot = gate_both[count:]
    upper = up_both[:count]
    up_dot = up_both[count:]
    back = lax.dot_general(
        rows_c, down_w, (((1,), (1,)), ((), ())), preferred_element_type=jnp.float32
    )
    back = back * rows_w.astype(jnp.float32)[:, None]
    sigma = jax.nn.sigmoid(gate)
    first = sigma * (1.0 + gate * (1.0 - sigma))
    second = sigma * (1.0 - sigma) * (2.0 + gate * (1.0 - 2.0 * sigma))
    gate_change = (back * (up_dot * first + upper * second * gate_dot)).astype(jnp.bfloat16)
    up_change = (back * first * gate_dot).astype(jnp.bfloat16)
    term = lax.dot_general(
        gate_change, gate_w, (((1,), (1,)), ((), ())), preferred_element_type=jnp.float32
    )
    term = term + lax.dot_general(
        up_change, up_w, (((1,), (1,)), ((), ())), preferred_element_type=jnp.float32
    )
    return term.astype(jnp.bfloat16)


def shards(tokens, tangent, cotangent, routes, route_weight, gate_weight, up_weight, down_weight):
    experts = lax.axis_size("expert")
    tok_rows, width = tokens.shape
    top_count = routes.shape[1]
    slots = 2 * tok_rows * top_count // experts
    if slots >= tok_rows and experts == 4 * LINES:
        return whole_blocks(
            tokens, tangent, cotangent, routes, route_weight, gate_weight, up_weight, down_weight
        )
    routed = tok_rows * top_count
    flat_routes = routes.reshape(-1)
    onehot = (flat_routes[:, None] == jnp.arange(experts, dtype=jnp.int32)[None, :]).astype(
        jnp.int32
    )
    slot_rank = jnp.sum((jnp.cumsum(onehot, axis=0) - onehot) * onehot, axis=1)
    target = flat_routes * slots + slot_rank
    source = (
        jnp.zeros((experts * slots,), jnp.int32).at[target].set(jnp.arange(routed, dtype=jnp.int32))
    )
    filled = jnp.zeros((experts * slots,), jnp.bool_).at[target].set(True)
    owner = source // top_count

    def place(values):
        picked = jnp.where(filled[:, None], values[owner], jnp.zeros((), values.dtype))
        return picked.reshape(experts, slots, width)

    send_x = place(tokens)
    send_v = place(tangent)
    send_c = place(cotangent)
    send_w = jnp.where(
        filled, route_weight.reshape(-1)[source], jnp.zeros((), route_weight.dtype)
    ).reshape(experts, slots)
    gate_w = gate_weight[0]
    up_w = up_weight[0]
    down_w = down_weight[0]
    recv_w = lax.all_to_all(send_w, "expert", split_axis=0, concat_axis=0, tiled=True)
    sources, levels = recv_w.shape
    result = route_terms(
        lax.all_to_all(send_x, "expert", split_axis=0, concat_axis=0, tiled=True).reshape(
            -1, width
        ),
        lax.all_to_all(send_v, "expert", split_axis=0, concat_axis=0, tiled=True).reshape(
            -1, width
        ),
        lax.all_to_all(send_c, "expert", split_axis=0, concat_axis=0, tiled=True).reshape(
            -1, width
        ),
        recv_w.reshape(-1),
        gate_w,
        up_w,
        down_w,
    )
    terms = result.reshape(sources, levels, width)
    returned = lax.all_to_all(terms, "expert", split_axis=0, concat_axis=0, tiled=True)
    back_flat = returned.reshape(experts * slots, width)
    per_route = back_flat[target].astype(jnp.float32).reshape(tok_rows, top_count, width)
    return jnp.sum(per_route, axis=1)


def solution(mesh):
    placed = (
        P(("groups", "expert"), None),
        P(("groups", "expert"), None),
        P(("groups", "expert"), None),
        P(("groups", "expert"), None),
        P(("groups", "expert"), None),
        P("expert", None, None),
        P("expert", None, None),
        P("expert", None, None),
    )
    return jax.shard_map(
        shards, mesh=mesh, in_specs=placed, out_specs=P(("groups", "expert"), None), check_vma=False
    )
```
